512 devices in a mesh: video: 16 (over x_hi, y, core), seq: 32 (over z, x_lo).
Axes of the slice: x: 4 (x_hi: 2, x_lo: 2; x = x_hi * 2 + x_lo), y: 4, z: 16, core: 2. Of those that a mesh axis runs over, the one named last changes fastest.
Arguments:
- queries: bfloat16 [262144, 1152], P(('video', 'seq')), parts along dimension 0, may hold values from -6 to 6
- key_vectors: bfloat16 [262144, 1152], P(('video', 'seq')), parts along dimension 0, may hold values from -6 to 6
- values_in: bfloat16 [262144, 1152], P(('video', 'seq')), parts along dimension 0, may hold values from -6 to 6
- norm_gain: float32 [1152], replicated, may hold values from 0.1 to 1.9
- state_weight: bfloat16 [1152, 256], replicated, may hold values from -0.1875 to 0.1875
- step_weight: bfloat16 [1152, 32], replicated, may hold values from -0.1875 to 0.1875
- step_bias: float32 [32], replicated, may hold values from -1 to 1
- decay_rate: float32 [32], replicated, may hold values from 0.005 to 0.2
Outputs:
- block_output: bfloat16 [262144, 1152], P(('video', 'seq')), parts along dimension 0
The draws below stay inside these ranges and needn't reach their ends.
There are 16 independent parts, one for each index of `video`. The reference program is written for one: setup_inputs(seed, part) draws one part's arguments, and reference() takes and returns one part's arrays. A program takes and returns all parts, laid end to end along the dimension named above; an argument that names none is the same for every part. Nothing has to cross between parts.
All inputs are finite; a program needn't handle non-finite values.
Results may differ from the reference program's by a relative error of at most 0.011.
Values may be sent and summed in bfloat16 or wider, within the bound.
A program may use at most 64 MiB of HBM per device.

```python
import math
import jax
import jax.numpy as jnp
from jax import lax

HEADS = 16
HEAD = 72
STATE = 64
D = 1152
P_SIZE = 512
FRAMES = 32
TOKENS = 16384


def draw_queries(key, part):
    key = jax.random.fold_in(key, 5)
    base_draw = jnp.clip(jax.random.normal(key, (FRAMES, P_SIZE, D), jnp.float32), -6.0, 6.0)
    return base_draw.reshape(FRAMES * P_SIZE, D).astype(jnp.bfloat16)


def draw_key_vectors(key, part):
    key = jax.random.fold_in(key, 9)
    base_draw = jnp.clip(jax.random.normal(key, (FRAMES, P_SIZE, D), jnp.float32), -6.0, 6.0)
    return base_draw.reshape(FRAMES * P_SIZE, D).astype(jnp.bfloat16)


def block_levels(own_key, extent, shards, smallest, high):
    def one(position, blocks):
        draws = jax.random.uniform(jax.random.fold_in(jax.random.fold_in(own_key, 6), position), (blocks,), jnp.float32, smallest / len(shards), high / len(shards))
        return jnp.repeat(jnp.exp(draws), extent[position] // blocks).reshape((-1,) + (1,) * (len(extent) - position - 1))

    loudness = one(*shards[0])
    for cut in shards[1:]:
        loudness = loudness * one(*cut)
    return loudness


def normal_values(rng, dims, width, bound, shards=(), kind=jnp.bfloat16):
    gain = block_levels(rng, dims, shards, -0.22, 0.18) if shards else 1.0
    values = jax.random.normal(rng, dims, jnp.float32) * width * gain
    return jnp.minimum(jnp.maximum(values, -bound), bound).astype(kind)


def setup_inputs(seed: int = 0, part: int = 0) -> dict:
    streams_of = jax.random.split(jax.random.key(seed), 9)
    own_keys = jax.random.split(jax.random.fold_in(streams_of[8], part), 9)
    queries = draw_queries(jax.random.fold_in(jax.random.fold_in(streams_of[8], part), 71), part)
    key_vectors = draw_key_vectors(jax.random.fold_in(jax.random.fold_in(streams_of[8], part), 71), part)
    values_in = normal_values(own_keys[2], (TOKENS, D), 1.0, 6.0, ((0, 32),))
    norm_gain = jnp.clip(1.0 + 0.18 * jax.random.normal(streams_of[3], (D,), jnp.float32), 0.1, 1.9)
    state_weight = normal_values(streams_of[4], (D, 4 * STATE), D ** -0.5, 0.1875)
    step_weight = normal_values(streams_of[5], (D, 2 * HEADS), D ** -0.5, 0.1875)
    step_bias = jnp.clip(jax.random.uniform(streams_of[6], (2 * HEADS,), jnp.float32, -1.0, 1.0), -1.0, 1.0)
    decay_rate = jnp.clip(jnp.exp(jax.random.uniform(streams_of[7], (2 * HEADS,), jnp.float32, math.log(0.005), math.log(0.2))), 0.005, 0.2)
    return {"queries": queries, "key_vectors": key_vectors, "values_in": values_in, "norm_gain": norm_gain, "state_weight": state_weight, "step_weight": step_weight, "step_bias": step_bias, "decay_rate": decay_rate}


EPSILON = 1e-06

def attend_frame(frame_inputs):
    query_rows, key_rows, value_rows = frame_inputs
    tokens = query_rows.shape[0]
    query_heads = query_rows.astype(jnp.float32).reshape(tokens, HEADS, HEAD)
    key_heads = key_rows.astype(jnp.float32).reshape(tokens, HEADS, HEAD)
    value_heads = value_rows.astype(jnp.float32).reshape(tokens, HEADS, HEAD)
    scores = jnp.einsum('qhe,khe->hqk', query_heads, key_heads) * HEAD ** (-0.5)
    row_max = lax.optimization_barrier(jnp.max(scores, axis=-1, keepdims=True))
    exponent = jnp.exp(scores - row_max)
    probabilities = (exponent / lax.optimization_barrier(jnp.sum(exponent, axis=-1, keepdims=True))).astype(jnp.bfloat16)
    attended = jnp.einsum('hqk,khe->qhe', probabilities.astype(jnp.float32), value_heads)
    return attended.reshape(tokens, HEADS * HEAD).astype(jnp.bfloat16)

def normalize(attended, norm_gain):
    widened = attended.astype(jnp.float32)
    mean_square = lax.optimization_barrier(jnp.mean(widened * widened, axis=-1, keepdims=True))
    return (widened * lax.rsqrt(mean_square + EPSILON) * norm_gain).astype(jnp.bfloat16)

def temporal_mix(normed, state_proj, step_proj, step_bias, decay_rate):
    frames, patches, channels = normed.shape
    head_count = step_proj.shape[2] // 2
    state_size = state_proj.shape[2] // 4
    step_size = jax.nn.softplus(step_proj.astype(jnp.float32) + step_bias)
    forward_step = step_size[..., :head_count]
    backward_step = step_size[..., head_count:]
    forward_total = jnp.cumsum(forward_step, axis=0)
    backward_total = jnp.flip(jnp.cumsum(jnp.flip(backward_step, 0), axis=0), 0)
    projected = state_proj.astype(jnp.float32)
    input_fwd = projected[..., :state_size]
    output_fwd = projected[..., state_size:2 * state_size]
    input_bwd = projected[..., 2 * state_size:3 * state_size]
    output_bwd = projected[..., 3 * state_size:]
    gram_forward = jnp.einsum('tpn,spn->pts', output_fwd, input_fwd) * state_size ** (-0.5)
    gram_backward = jnp.einsum('tpn,spn->pts', output_bwd, input_bwd) * state_size ** (-0.5)
    positions = jnp.arange(frames)
    causal_mask = positions[:, None] >= positions[None, :]
    anti_mask = positions[:, None] <= positions[None, :]
    forward_lead = jnp.transpose(forward_total, (1, 2, 0))
    backward_lead = jnp.transpose(backward_total, (1, 2, 0))
    forward_gap = forward_lead[..., :, None] - forward_lead[..., None, :]
    backward_gap = backward_lead[..., :, None] - backward_lead[..., None, :]
    forward_decay = jnp.where(causal_mask, jnp.exp(-decay_rate[:head_count, None, None] * jnp.where(causal_mask, forward_gap, 0.0)), 0.0)
    backward_decay = jnp.where(anti_mask, jnp.exp(-decay_rate[head_count:, None, None] * jnp.where(anti_mask, backward_gap, 0.0)), 0.0)
    forward_weight = gram_forward[:, None] * forward_decay * jnp.transpose(forward_step, (1, 2, 0))[:, :, None, :]
    backward_weight = gram_backward[:, None] * backward_decay * jnp.transpose(backward_step, (1, 2, 0))[:, :, None, :]
    scan_weights = (forward_weight + backward_weight).astype(jnp.bfloat16)
    normed_heads = normed.astype(jnp.float32).reshape(frames, patches, head_count, channels // head_count)
    carried = jnp.einsum('phts,sphe->tphe', scan_weights.astype(jnp.float32), normed_heads)
    return (normed.astype(jnp.float32) + carried.reshape(frames, patches, channels)).astype(jnp.bfloat16)

def reference(queries, key_vectors, values_in, norm_gain, state_weight, step_weight, step_bias, decay_rate):
    channels = queries.shape[1]
    attended = lax.map(attend_frame, (queries.reshape(FRAMES, P_SIZE, channels), key_vectors.reshape(FRAMES, P_SIZE, channels), values_in.reshape(FRAMES, P_SIZE, channels)))
    normed = normalize(attended, norm_gain)
    flat_normed = normed.reshape(FRAMES * P_SIZE, channels)
    state_proj = jnp.dot(flat_normed, state_weight, preferred_element_type=jnp.float32).astype(jnp.bfloat16).reshape(FRAMES, P_SIZE, -1)
    step_proj = jnp.dot(flat_normed, step_weight, preferred_element_type=jnp.float32).astype(jnp.bfloat16).reshape(FRAMES, P_SIZE, -1)
    mixed = temporal_mix(normed, state_proj, step_proj, step_bias, decay_rate)
    return mixed.reshape(FRAMES * P_SIZE, channels)
```

```python
import functools

import jax
import jax.numpy as jnp
from jax import lax
from jax.experimental import pallas as pl
from jax.experimental.pallas import tpu as pltpu
from jax.sharding import PartitionSpec as P

HEADS = 16
HEAD = 72
STATE = 64
EPSILON = 1e-06
LOG2E = 1.4426950408889634
WINDOW = 256
MESH = pl.DeviceIdType.MESH
F32 = jnp.float32
BF16 = jnp.bfloat16


def window_of(head, channels):
    start = head * HEAD // 128 * 128
    if isinstance(head, int):
        start = min(start, channels - WINDOW)
    else:
        start = pl.multiple_of(jnp.minimum(start, channels - WINDOW), 128)
    return start, head * HEAD - start


def head_mask(rows, offset):
    lane = lax.broadcasted_iota(jnp.int32, (rows, WINDOW), 1)
    return (lane >= offset) & (lane < offset + HEAD)


def attend(q_ref, k_ref, v_ref, acc_ref, row, unroll):
    rows, channels = acc_ref.shape
    scale = HEAD ** (-0.5) * LOG2E

    def one_head(head, carry):
        start, offset = window_of(head, channels)
        lanes = pl.ds(start, WINDOW)
        mask = head_mask(rows, offset)
        query = jnp.where(mask, q_ref[pl.ds(row, rows), lanes], jnp.zeros((), BF16))
        scores = lax.dot_general(
            query, k_ref[:, lanes], (((1,), (1,)), ((), ())), preferred_element_type=F32
        )
        row_max = jnp.max(scores, axis=1, keepdims=True)
        exponent = jnp.exp2((scores - row_max) * scale)
        total = jnp.sum(exponent, axis=1, keepdims=True)
        mixed = jnp.dot(exponent.astype(BF16), v_ref[:, lanes], preferred_element_type=F32)
        acc_ref[:, lanes] = jnp.where(mask, mixed * (1.0 / total), acc_ref[:, lanes])
        return carry

    lax.fori_loop(0, HEADS, one_head, 0, unroll=unroll)


def normalize(attended, gain):
    widened = attended.astype(BF16).astype(F32)
    mean_square = jnp.mean(widened * widened, axis=1, keepdims=True)
    return (widened * lax.rsqrt(mean_square + EPSILON) * gain).astype(BF16)


def prepare_group(group, x_ref, xb_ref, sw_ref, tw_ref, bias_ref, decay_ref, gram_ref, lead_ref, lead_t_ref, step_t_ref):
    rows = gram_ref.shape[2]
    frames = rows // 4
    base = pl.multiple_of(group * rows, rows)
    for tile in range(x_ref.shape[0]):
        xb_ref[pl.ds(base, rows), pl.ds(tile * 128, 128)] = x_ref[tile, pl.ds(base, rows), :].astype(BF16)
    normed = xb_ref[pl.ds(base, rows), :]
    state = jnp.dot(normed, sw_ref[...], preferred_element_type=F32).astype(BF16)
    step = jnp.dot(normed, tw_ref[...], preferred_element_type=F32).astype(BF16).astype(F32)
    step = step + bias_ref[...]
    step = jnp.maximum(step, 0.0) + jnp.log1p(jnp.exp(-jnp.abs(step)))
    i = lax.broadcasted_iota(jnp.int32, (rows, rows), 0)
    j = lax.broadcasted_iota(jnp.int32, (rows, rows), 1)
    same = (i // frames) == (j // frames)
    causal, anti = same & (j <= i), same & (j >= i)
    nt = (((1,), (1,)), ((), ()))
    for direction, mask in ((0, causal), (1, anti)):
        lo = 2 * STATE * direction
        gram = lax.dot_general(
            state[:, lo + STATE : lo + 2 * STATE], state[:, lo : lo + STATE], nt, preferred_element_type=F32
        )
        gram_ref[group, direction] = jnp.where(mask, gram * STATE ** (-0.5), 0.0)
    hi = step.astype(BF16)
    low = (step - hi.astype(F32)).astype(BF16)
    sums = []
    for mask in (causal, anti):
        ones = jnp.where(mask, 1.0, 0.0).astype(BF16)
        sums.append(
            jnp.dot(ones, hi, preferred_element_type=F32) + jnp.dot(ones, low, preferred_element_type=F32)
        )
    column = lax.broadcasted_iota(jnp.int32, step.shape, 1)
    lead = jnp.where(column < HEADS, sums[0], sums[1]) * (decay_ref[...] * LOG2E)
    lead_ref[group] = lead
    lead_t_ref[group] = lead.T
    step_t_ref[group] = step.T


def mix_group(group, heads, xb_ref, y_ref, gram_ref, lead_ref, lead_t_ref, step_t_ref):
    rows = gram_ref.shape[2]
    channels = xb_ref.shape[1]
    base = pl.multiple_of(group * rows, rows)
    i = lax.broadcasted_iota(jnp.int32, (rows, rows), 0)
    j = lax.broadcasted_iota(jnp.int32, (rows, rows), 1)
    causal = j <= i
    for head in heads:
        back = HEADS + head
        gap = jnp.where(
            causal,
            lead_t_ref[group, head : head + 1, :] - lead_ref[group, :, head : head + 1],
            lead_t_ref[group, back : back + 1, :] - lead_ref[group, :, back : back + 1],
        )
        weight = jnp.exp2(jnp.minimum(gap, 0.0)) * (
            gram_ref[group, 0] * step_t_ref[group, head : head + 1, :]
            + gram_ref[group, 1] * step_t_ref[group, back : back + 1, :]
        )
        start, offset = window_of(head, channels)
        lanes = pl.ds(start, WINDOW)
        normed = xb_ref[pl.ds(base, rows), lanes]
        mixed = jnp.dot(weight.astype(BF16), normed, preferred_element_type=F32) + normed.astype(F32)
        mask = head_mask(rows, offset)
        for side in range(WINDOW // 128):
            own = slice(side * 128, side * 128 + 128)
            if offset < own.stop and offset + HEAD > own.start:
                place = (start // 128 + side, pl.ds(base, rows), slice(None))
                y_ref[place] = jnp.where(mask[:, own], mixed[:, own], y_ref[place])


def kernel(
    frames, chunks,
    q_hbm, k_hbm, v_hbm, gain_ref, sw_ref, tw_ref, bias_ref, decay_ref, o_ref,
    q_ref, k_ref, v_ref, acc_ref, out1_ref, in1_ref, x_ref, xb_ref, y_ref, gram_ref, lead_ref, lead_t_ref, step_t_ref, out2_ref,
    in_sem, send1, recv1, send2, recv2, own_sem,
):
    video, me = lax.axis_index("video"), lax.axis_index("seq")
    tokens, channels = out1_ref.shape
    per = tokens // frames
    half = frames // 2
    block = acc_ref.shape[0]

    loads = [
        pltpu.make_async_copy(source, target, in_sem.at[n])
        for n, (source, target) in enumerate(((q_hbm, q_ref), (k_hbm, k_ref), (v_hbm, v_ref)))
    ]
    for load in loads:
        load.start()
    barrier = pltpu.get_barrier_semaphore()

    def greet(k, carry):
        pl.semaphore_signal(
            barrier, inc=1, device_id=(video, lax.rem(me + k, frames)), device_id_type=MESH
        )
        return carry

    lax.fori_loop(1, frames, greet, 0)
    for load in loads:
        load.wait()

    def rows_of(index):
        return pl.ds(pl.multiple_of(index * per, per), per)

    def first_copy(target):
        return pltpu.make_async_remote_copy(
            src_ref=out1_ref.at[rows_of(target)],
            dst_ref=in1_ref.at[rows_of(me)],
            send_sem=send1.at[target],
            recv_sem=recv1.at[me],
            device_id=(video, target),
            device_id_type=MESH,
        )

    def first_arrival(source):
        return pltpu.make_async_remote_copy(
            src_ref=out1_ref.at[rows_of(source)],
            dst_ref=in1_ref.at[rows_of(source)],
            send_sem=send1.at[source],
            recv_sem=recv1.at[source],
            device_id=(video, source),
            device_id_type=MESH,
        )

    for turn in range(2):
        side = lax.rem(me // half + 1 + turn, 2)
        row = pl.multiple_of(side * block, block)
        attend(q_ref, k_ref, v_ref, acc_ref, row, 4)
        out1_ref[pl.ds(row, block), :] = normalize(acc_ref[...], gain_ref[...])
        if turn == 0:
            pl.semaphore_wait(barrier, frames - 1)

        def send(k, carry, side=side):
            first_copy(side * half + lax.rem(me + k, half)).start()
            return carry

        lax.fori_loop(turn, half, send, 0)

    def place_rows(rows, source):
        rows = rows.astype(F32)
        for tile in range(channels // 128):
            x_ref[tile, pl.ds(source, per, stride=frames), :] = rows[:, tile * 128 : tile * 128 + 128]

    def spread(source):
        place_rows(in1_ref[rows_of(source), :], source)

    place_rows(out1_ref[rows_of(me), :], me)
    for turn in range(2):
        side = lax.rem(me // half + 1 + turn, 2)

        def arrive(k, carry, side=side):
            source = side * half + lax.rem(me + half - k, half)
            first_arrival(source).wait_recv()
            spread(source)
            return carry

        lax.fori_loop(turn, half, arrive, 0)

    groups = gram_ref.shape[0]

    def prepare(group, carry):
        prepare_group(
            group, x_ref, xb_ref, sw_ref, tw_ref, bias_ref, decay_ref, gram_ref, lead_ref, lead_t_ref, step_t_ref
        )
        return carry

    lax.fori_loop(0, groups, prepare, 0)

    def second_copy(n, target):
        lanes = pl.ds(chunks[n][0], chunks[n][1])
        return pltpu.make_async_remote_copy(
            src_ref=out2_ref.at[rows_of(target), lanes],
            dst_ref=o_ref.at[rows_of(me), lanes],
            send_sem=send2.at[n, target],
            recv_sem=recv2.at[n, me],
            device_id=(video, target),
            device_id_type=MESH,
        )

    def second_arrival(n, source):
        lanes = pl.ds(chunks[n][0], chunks[n][1])
        return pltpu.make_async_remote_copy(
            src_ref=out2_ref.at[rows_of(source), lanes],
            dst_ref=o_ref.at[rows_of(source), lanes],
            send_sem=send2.at[n, source],
            recv_sem=recv2.at[n, source],
            device_id=(video, source),
            device_id_type=MESH,
        )

    done = 0
    for n, (first, width) in enumerate(chunks):
        until = -(-(first + width) // HEAD)

        def mix(group, carry, heads=tuple(range(done, until))):
            mix_group(group, heads, xb_ref, y_ref, gram_ref, lead_ref, lead_t_ref, step_t_ref)
            return carry

        lax.fori_loop(0, groups, mix, 0)
        done = until

        def gather(target, first=first, width=width):
            for lane in range(first, first + width, 128):
                out2_ref[rows_of(target), pl.ds(lane, 128)] = y_ref[
                    lane // 128, pl.ds(target, per, stride=frames), :
                ].astype(BF16)

        for turn in range(2):
            side = lax.rem(me // half + 1 + turn, 2)

            def give(k, carry, side=side, n=n, gather=gather):
                target = side * half + lax.rem(me + k, half)
                gather(target)
                second_copy(n, target).start()
                return carry

            lax.fori_loop(turn, half, give, 0)
        gather(me)

    own = pltpu.make_async_copy(out2_ref.at[rows_of(me)], o_ref.at[rows_of(me)], own_sem)
    own.start()

    def sent1(k, carry):
        first_copy(lax.rem(me + k, frames)).wait_send()
        return carry

    lax.fori_loop(1, frames, sent1, 0)
    for n in range(len(chunks)):

        def finish(k, carry, n=n):
            second_copy(n, lax.rem(me + k, frames)).wait_send()
            second_arrival(n, lax.rem(me + k, frames)).wait_recv()
            return carry

        lax.fori_loop(1, frames, finish, 0)
    own.wait()


def shards(queries, key_vectors, values_in, norm_gain, state_weight, step_weight, step_bias, decay_rate):
    tokens, channels = queries.shape
    frames = lax.axis_size("seq")
    rows = 4 * frames
    groups = tokens // rows
    block = tokens // 2
    chunks = ((0, 128), (128, 256), (384, 384), (768, 384))
    vmem = pl.BlockSpec(memory_space=pltpu.VMEM)
    hbm = pl.BlockSpec(memory_space=pl.ANY)
    return pl.pallas_call(
        functools.partial(kernel, frames, chunks),
        out_shape=jax.ShapeDtypeStruct((tokens, channels), BF16),
        in_specs=[hbm, hbm, hbm, vmem, vmem, vmem, vmem, vmem],
        out_specs=hbm,
        scratch_shapes=[
            pltpu.VMEM((tokens, channels), BF16),
            pltpu.VMEM((tokens, channels), BF16),
            pltpu.VMEM((tokens, channels), BF16),
            pltpu.VMEM((block, channels), F32),
            pltpu.VMEM((tokens, channels), BF16),
            pltpu.VMEM((tokens, channels), BF16),
            pltpu.VMEM((channels // 128, tokens, 128), F32),
            pltpu.VMEM((tokens, channels), BF16),
            pltpu.VMEM((channels // 128, tokens, 128), F32),
            pltpu.VMEM((groups, 2, rows, rows), F32),
            pltpu.VMEM((groups, rows, 2 * HEADS), F32),
            pltpu.VMEM((groups, 2 * HEADS, rows), F32),
            pltpu.VMEM((groups, 2 * HEADS, rows), F32),
            pltpu.VMEM((tokens, channels), BF16),
            pltpu.SemaphoreType.DMA((3,)),
            pltpu.SemaphoreType.DMA((frames,)),
            pltpu.SemaphoreType.DMA((frames,)),
            pltpu.SemaphoreType.DMA((len(chunks), frames)),
            pltpu.SemaphoreType.DMA((len(chunks), frames)),
            pltpu.SemaphoreType.DMA,
        ],
        compiler_params=pltpu.CompilerParams(
            collective_id=0, has_side_effects=True, vmem_limit_bytes=48 * 2**20
        ),
    )(
        queries, key_vectors, values_in, norm_gain[None], state_weight, step_weight, step_bias[None], decay_rate[None]
    )


def solution(mesh):
    rows = P(("video", "seq"), None)
    return jax.shard_map(
        shards,
        mesh=mesh,
        in_specs=(rows, rows, rows, P(), P(), P(), P(), P()),
        out_specs=rows,
        check_vma=False,
    )
```

```python
import functools

import jax
import jax.numpy as jnp
from jax import lax
from jax.experimental import pallas as pl
from jax.experimental.pallas import tpu as pltpu
from jax.sharding import PartitionSpec as P

HEADS = 16
HEAD = 72
STATE = 64
EPSILON = 1e-06
LOG2E = 1.4426950408889634
WINDOW = 256
MESH = pl.DeviceIdType.MESH
NT = (((1,), (1,)), ((), ()))
F32 = jnp.float32
BF16 = jnp.bfloat16


def window_of(head, channels):
    start = min(head * HEAD // 128 * 128, channels - WINDOW)
    return start, head * HEAD - start


def head_mask(rows, offset):
    lane = lax.broadcasted_iota(jnp.int32, (rows, WINDOW), 1)
    return (lane >= offset) & (lane < offset + HEAD)


def attend(q_ref, k_ref, v_ref, acc_ref, row):
    rows, channels = acc_ref.shape
    scale = HEAD ** (-0.5) * LOG2E
    for head in range(HEADS):
        start, offset = window_of(head, channels)
        lanes = pl.ds(start, WINDOW)
        mask = head_mask(rows, offset)
        query = jnp.where(mask, q_ref[pl.ds(row, rows), lanes], jnp.zeros((), BF16))
        scores = lax.dot_general(query, k_ref[:, lanes], NT, preferred_element_type=F32)
        row_max = jnp.max(scores, axis=1, keepdims=True)
        exponent = jnp.exp2((scores - row_max) * scale)
        total = jnp.sum(exponent, axis=1, keepdims=True)
        probabilities = (exponent * (1.0 / total)).astype(BF16)
        mixed = jnp.dot(probabilities, v_ref[:, lanes], preferred_element_type=F32)
        acc_ref[:, lanes] = jnp.where(mask, mixed, acc_ref[:, lanes])


def normalize(attended, gain):
    widened = attended.astype(BF16).astype(F32)
    mean_square = jnp.mean(widened * widened, axis=1, keepdims=True)
    return (widened * lax.rsqrt(mean_square + EPSILON) * gain).astype(BF16)


def prepare_group(group, proj_ref, bias_ref, decay_ref, gram_ref, lead_ref, lead_t_ref, step_t_ref):
    rows = gram_ref.shape[2]
    frames = rows // 4
    base = pl.ds(pl.multiple_of(group * rows, rows), rows)
    i = lax.broadcasted_iota(jnp.int32, (rows, rows), 0)
    j = lax.broadcasted_iota(jnp.int32, (rows, rows), 1)
    same = (i // frames) == (j // frames)
    causal, anti = same & (j <= i), same & (j >= i)
    for direction, mask in ((0, causal), (1, anti)):
        state = proj_ref[direction, base, :].astype(BF16)
        gram = lax.dot_general(state[:, STATE:], state[:, :STATE], NT, preferred_element_type=F32)
        gram_ref[group, direction] = jnp.where(mask, gram * STATE ** (-0.5), 0.0)
    step = proj_ref[2, base, : 2 * HEADS] + bias_ref[...]
    step = jnp.maximum(step, 0.0) + jnp.log1p(jnp.exp(-jnp.abs(step)))
    high = step.astype(BF16)
    low = (step - high.astype(F32)).astype(BF16)
    sums = []
    for mask in (causal, anti):
        ones = jnp.where(mask, 1.0, 0.0).astype(BF16)
        sums.append(
            jnp.dot(ones, high, preferred_element_type=F32) + jnp.dot(ones, low, preferred_element_type=F32)
        )
    column = lax.broadcasted_iota(jnp.int32, step.shape, 1)
    lead = jnp.where(column < HEADS, sums[0], sums[1]) * (decay_ref[...] * LOG2E)
    lead_ref[group] = lead
    lead_t_ref[group] = lead.T
    step_t_ref[group] = step.T


def mix_group(group, heads, tiles, x_ref, xb_ref, y_ref, gram_ref, lead_ref, lead_t_ref, step_t_ref):
    rows = gram_ref.shape[2]
    channels = xb_ref.shape[1]
    base = pl.ds(pl.multiple_of(group * rows, rows), rows)
    for tile in tiles:
        xb_ref[base, pl.ds(tile * 128, 128)] = x_ref[tile, base, :].astype(BF16)
    i = lax.broadcasted_iota(jnp.int32, (rows, rows), 0)
    j = lax.broadcasted_iota(jnp.int32, (rows, rows), 1)
    causal = j <= i
    for head in heads:
        back = HEADS + head
        gap = jnp.where(
            causal,
            lead_t_ref[group, head : head + 1, :] - lead_ref[group, :, head : head + 1],
            lead_t_ref[group, back : back + 1, :] - lead_ref[group, :, back : back + 1],
        )
        weight = jnp.exp2(jnp.minimum(gap, 0.0)) * (
            gram_ref[group, 0] * step_t_ref[group, head : head + 1, :]
            + gram_ref[group, 1] * step_t_ref[group, back : back + 1, :]
        )
        start, offset = window_of(head, channels)
        normed = xb_ref[base, pl.ds(start, WINDOW)]
        mixed = jnp.dot(weight.astype(BF16), normed, preferred_element_type=F32) + normed.astype(F32)
        mask = head_mask(rows, offset)
        for side in range(WINDOW // 128):
            own = slice(side * 128, side * 128 + 128)
            if offset < own.stop and offset + HEAD > own.start:
                place = (start // 128 + side, base, slice(None))
                y_ref[place] = jnp.where(mask[:, own], mixed[:, own], y_ref[place])


def kernel(
    frames, chunks,
    q_hbm, k_hbm, v_hbm, sw_hbm, tw_hbm, gain_ref, bias_ref, decay_ref, o_ref,
    q_ref, k_ref, v_ref, sw_ref, tw_ref, acc_ref, out1_ref, in1_ref, x_ref, xb_ref, y_ref, proj_ref,
    gram_ref, lead_ref, lead_t_ref, step_t_ref, out2_ref,
    q_sem, in_sem, send1, recv1, send2, recv2, own_sem,
):
    video, me = lax.axis_index("video"), lax.axis_index("seq")
    tokens, channels = out1_ref.shape
    per = tokens // frames
    ring = frames // 2
    my_ring, my_side = me // 2, lax.rem(me, 2)
    block = acc_ref.shape[0]
    tiles = channels // 128

    half = ring // 2
    my_parity = lax.rem(my_ring, 2)

    def shift(place):
        return half + jnp.where(lax.rem(place, 2) == 0, place // 2, -((place + 1) // 2))

    def device_at(distance, side):
        return 2 * lax.rem(my_ring + distance, ring) + side

    def peer(n):
        return device_at(shift(n // 2), lax.rem(n, 2))

    def slot_at(distance):
        back = lax.rem(ring - distance, ring)
        place = jnp.where(back >= half, 2 * (back - half), 2 * (half - back) - 1)
        return 2 * place + my_side

    def first_shift(place):
        step = lax.rem(place, half)
        up = lax.rem(step + place // half + my_parity, 2) == 0
        return jnp.where(up, half + step, half - 1 - step)

    def rows_of(index):
        return pl.ds(pl.multiple_of(index * per, per), per)

    def load_queries(place):
        rows = 2 * per
        source = lax.rem(my_ring + first_shift(place), ring)
        return pltpu.make_async_copy(
            q_hbm.at[pl.ds(pl.multiple_of(source * rows, rows), rows)],
            q_ref.at[pl.ds(pl.multiple_of(place * rows, rows), rows)],
            q_sem.at[place],
        )

    def each(low, high, body):
        def step(n, carry):
            body(n)
            return carry

        lax.fori_loop(low, high, step, 0)

    loads = [
        pltpu.make_async_copy(source, target, in_sem.at[n])
        for n, (source, target) in enumerate(
            ((k_hbm, k_ref), (v_hbm, v_ref), (sw_hbm, sw_ref), (tw_hbm, tw_ref))
        )
    ]
    loads[0].start()
    each(0, ring, lambda place: load_queries(place).start())
    for load in loads[1:]:
        load.start()
    barrier = pltpu.get_barrier_semaphore()
    each(
        1,
        frames,
        lambda k: pl.semaphore_signal(
            barrier, inc=1, device_id=(video, lax.rem(me + k, frames)), device_id_type=MESH
        ),
    )
    each(0, ring, lambda place: load_queries(place).wait())
    for load in loads:
        load.wait()

    def first_copy(n):
        distance = first_shift(n // 2)
        there = slot_at(distance)
        return pltpu.make_async_remote_copy(
            src_ref=out1_ref.at[rows_of(n)],
            dst_ref=in1_ref.at[rows_of(there)],
            send_sem=send1.at[n],
            recv_sem=recv1.at[there],
            device_id=(video, device_at(distance, lax.rem(n, 2))),
            device_id_type=MESH,
        )

    def first_arrival(n):
        return pltpu.make_async_remote_copy(
            src_ref=out1_ref.at[rows_of(n)],
            dst_ref=in1_ref.at[rows_of(n)],
            send_sem=send1.at[n],
            recv_sem=recv1.at[n],
            device_id=(video, peer(n)),
            device_id_type=MESH,
        )

    own_slot = frames - 2 + my_side
    own_first = 2 * (half * my_parity + half - 1) + my_side

    def remote(n, action, own=own_slot):
        @pl.when(n != own)
        def _():
            action(n)

    def remote_first(n, action):
        remote(n, action, own_first)

    per_block = block // per

    def first_part(turn):
        row = pl.multiple_of(turn * block, block)
        attend(q_ref, k_ref, v_ref, acc_ref, row)
        out1_ref[pl.ds(row, block), :] = normalize(acc_ref[...], gain_ref[...][None])

        @pl.when(turn == 0)
        def _():
            pl.semaphore_wait(barrier, frames - 1)

        each(turn * per_block, (turn + 1) * per_block, lambda n: remote_first(n, lambda n: first_copy(n).start()))

    each(0, tokens // block, first_part)
    in1_ref[rows_of(own_slot), :] = out1_ref[rows_of(own_first), :]

    groups, rows = gram_ref.shape[0], gram_ref.shape[2]

    def arrive(batch):
        for k in range(rows // per):
            n = batch * (rows // per) + k
            remote(n, lambda n: first_arrival(n).wait_recv())
        arrived = in1_ref[pl.ds(pl.multiple_of(batch * rows, rows), rows), :]
        state = jnp.dot(arrived, sw_ref[...], preferred_element_type=F32).astype(BF16).astype(F32)
        step = lax.dot_general(arrived, tw_ref[...], NT, preferred_element_type=F32).astype(BF16).astype(F32)
        for k in range(rows // per):
            n = batch * (rows // per) + k
            place = pl.ds(peer(n), per, stride=frames)
            here = slice(k * per, k * per + per)
            wide = in1_ref[rows_of(n), :].astype(F32)
            for tile in range(tiles):
                x_ref[tile, place, :] = wide[:, tile * 128 : tile * 128 + 128]
            proj_ref[0, place, :] = state[here, :128]
            proj_ref[1, place, :] = state[here, 128:]
            proj_ref[2, place, :] = jnp.concatenate([step[here]] * (128 // step.shape[1]), axis=1)

    each(0, groups, arrive)
    each(
        0,
        groups,
        lambda group: prepare_group(
            group, proj_ref, bias_ref, decay_ref, gram_ref, lead_ref, lead_t_ref, step_t_ref
        ),
    )

    def second_copy(c, n):
        lanes = pl.ds(chunks[c][0], chunks[c][1])
        return pltpu.make_async_remote_copy(
            src_ref=out2_ref.at[rows_of(n), lanes],
            dst_ref=o_ref.at[rows_of(me), lanes],
            send_sem=send2.at[c, n],
            recv_sem=recv2.at[c, slot_at(shift(n // 2))],
            device_id=(video, peer(n)),
            device_id_type=MESH,
        )

    def second_arrival(c, n):
        lanes = pl.ds(chunks[c][0], chunks[c][1])
        return pltpu.make_async_remote_copy(
            src_ref=out2_ref.at[rows_of(n), lanes],
            dst_ref=o_ref.at[rows_of(peer(n)), lanes],
            send_sem=send2.at[c, n],
            recv_sem=recv2.at[c, n],
            device_id=(video, peer(n)),
            device_id_type=MESH,
        )

    done, wide_done = 0, 0
    for c, (first, width) in enumerate(chunks):
        until = -(-(first + width) // HEAD)
        wide_until = (window_of(until - 1, channels)[0] + WINDOW) // 128
        heads, wide = range(done, until), range(wide_done, wide_until)
        done, wide_done = until, wide_until
        each(
            0,
            groups,
            lambda group, heads=heads, wide=wide: mix_group(
                group, heads, wide, x_ref, xb_ref, y_ref, gram_ref, lead_ref, lead_t_ref, step_t_ref
            ),
        )

        def give(n, c=c, first=first, width=width):
            for lane in range(first, first + width, 128):
                out2_ref[rows_of(n), pl.ds(lane, 128)] = y_ref[
                    lane // 128, pl.ds(peer(n), per, stride=frames), :
                ].astype(BF16)
            remote(n, lambda n: second_copy(c, n).start())

        each(0, frames, give)

    own = pltpu.make_async_copy(out2_ref.at[rows_of(own_slot)], o_ref.at[rows_of(me)], own_sem)
    own.start()
    each(0, frames, lambda n: remote_first(n, lambda n: first_copy(n).wait_send()))
    for c in range(len(chunks)):

        def finish(n, c=c):
            second_copy(c, n).wait_send()
            second_arrival(c, n).wait_recv()

        each(0, frames, lambda n, finish=finish: remote(n, finish))
    own.wait()


def shards(queries, key_vectors, values_in, norm_gain, state_weight, step_weight, step_bias, decay_rate):
    tokens, channels = queries.shape
    frames = lax.axis_size("seq")
    rows = 4 * frames
    groups = tokens // rows
    block = tokens // 2
    chunks = ((0, 128), (128, 256), (384, 384), (768, 384))
    vmem = pl.BlockSpec(memory_space=pltpu.VMEM)
    hbm = pl.BlockSpec(memory_space=pltpu.HBM)
    return pl.pallas_call(
        functools.partial(kernel, frames, chunks),
        out_shape=jax.ShapeDtypeStruct((tokens, channels), BF16),
        in_specs=[hbm, hbm, hbm, hbm, hbm, vmem, vmem, vmem],
        out_specs=pl.BlockSpec(memory_space=pl.ANY),
        scratch_shapes=[
            pltpu.VMEM((tokens, channels), BF16),
            pltpu.VMEM((tokens, channels), BF16),
            pltpu.VMEM((tokens, channels), BF16),
            pltpu.VMEM(state_weight.shape, BF16),
            pltpu.VMEM(step_weight.shape[::-1], BF16),
            pltpu.VMEM((block, channels), F32),
            pltpu.VMEM((tokens, channels), BF16),
            pltpu.VMEM((tokens, channels), BF16),
            pltpu.VMEM((channels // 128, tokens, 128), F32),
            pltpu.VMEM((tokens, channels), BF16),
            pltpu.VMEM((channels // 128, tokens, 128), F32),
            pltpu.VMEM((3, tokens, 128), F32),
            pltpu.VMEM((groups, 2, rows, rows), F32),
            pltpu.VMEM((groups, rows, 2 * HEADS), F32),
            pltpu.VMEM((groups, 2 * HEADS, rows), F32),
            pltpu.VMEM((groups, 2 * HEADS, rows), F32),
            pltpu.VMEM((tokens, channels), BF16),
            pltpu.SemaphoreType.DMA((frames // 2,)),
            pltpu.SemaphoreType.DMA((4,)),
            pltpu.SemaphoreType.DMA((frames,)),
            pltpu.SemaphoreType.DMA((frames,)),
            pltpu.SemaphoreType.DMA((len(chunks), frames)),
            pltpu.SemaphoreType.DMA((len(chunks), frames)),
            pltpu.SemaphoreType.DMA,
        ],
        compiler_params=pltpu.CompilerParams(
            collective_id=0, has_side_effects=True, vmem_limit_bytes=62 * 2**20
        ),
    )(
        queries, key_vectors, values_in, state_weight, step_weight.T, norm_gain, step_bias[None], decay_rate[None]
    )


def solution(mesh):
    rows = P(("video", "seq"), None)
    return jax.shard_map(
        shards,
        mesh=mesh,
        in_specs=(rows, rows, rows, P(), P(), P(), P(), P()),
        out_specs=rows,
        check_vma=False,
    )
```

```python
import functools

import jax
import jax.numpy as jnp
from jax import lax
from jax.experimental import pallas as pl
from jax.experimental.pallas import tpu as pltpu
from jax.sharding import PartitionSpec as P

HEADS = 16
HEAD = 72
STATE = 64
EPSILON = 1e-06
LOG2E = 1.4426950408889634
WINDOW = 256
MESH = pl.DeviceIdType.MESH
NT = (((1,), (1,)), ((), ()))
F32 = jnp.float32
BF16 = jnp.bfloat16


def window_of(head, channels):
    start = min(head * HEAD // 128 * 128, channels - WINDOW)
    return start, head * HEAD - start


def head_mask(rows, offset):
    lane = lax.broadcasted_iota(jnp.int32, (rows, WINDOW), 1)
    return (lane >= offset) & (lane < offset + HEAD)


def attend(q_ref, k_ref, v_ref, acc_ref, row):
    rows, channels = acc_ref.shape
    scale = HEAD ** (-0.5) * LOG2E
    for head in range(HEADS):
        start, offset = window_of(head, channels)
        lanes = pl.ds(start, WINDOW)
        mask = head_mask(rows, offset)
        query = jnp.where(mask, q_ref[pl.ds(row, rows), lanes], jnp.zeros((), BF16))
        scores = lax.dot_general(query, k_ref[:, lanes], NT, preferred_element_type=F32)
        row_max = jnp.max(scores, axis=1, keepdims=True)
        exponent = jnp.exp2((scores - row_max) * scale)
        total = jnp.sum(exponent, axis=1, keepdims=True)
        probabilities = (exponent * (1.0 / total)).astype(BF16)
        mixed = jnp.dot(probabilities, v_ref[:, lanes], preferred_element_type=F32)
        acc_ref[:, lanes] = jnp.where(mask, mixed, acc_ref[:, lanes])


def normalize(attended, gain):
    widened = attended.astype(BF16).astype(F32)
    mean_square = jnp.mean(widened * widened, axis=1, keepdims=True)
    return (widened * lax.rsqrt(mean_square + EPSILON) * gain).astype(BF16)


def prepare_group(group, proj_ref, bias_ref, decay_ref, gram_ref, lead_ref, lead_t_ref, step_t_ref):
    rows = gram_ref.shape[2]
    frames = rows // 4
    base = pl.ds(pl.multiple_of(group * rows, rows), rows)
    i = lax.broadcasted_iota(jnp.int32, (rows, rows), 0)
    j = lax.broadcasted_iota(jnp.int32, (rows, rows), 1)
    same = (i // frames) == (j // frames)
    causal, anti = same & (j <= i), same & (j >= i)
    for direction, mask in ((0, causal), (1, anti)):
        state = proj_ref[direction, base, :].astype(BF16)
        gram = lax.dot_general(state[:, STATE:], state[:, :STATE], NT, preferred_element_type=F32)
        gram_ref[group, direction] = jnp.where(mask, gram * STATE ** (-0.5), 0.0)
    step = proj_ref[2, base, : 2 * HEADS] + bias_ref[...]
    step = jnp.maximum(step, 0.0) + jnp.log1p(jnp.exp(-jnp.abs(step)))
    high = step.astype(BF16)
    low = (step - high.astype(F32)).astype(BF16)
    sums = []
    for mask in (causal, anti):
        ones = jnp.where(mask, 1.0, 0.0).astype(BF16)
        sums.append(
            jnp.dot(ones, high, preferred_element_type=F32) + jnp.dot(ones, low, preferred_element_type=F32)
        )
    column = lax.broadcasted_iota(jnp.int32, step.shape, 1)
    lead = jnp.where(column < HEADS, sums[0], sums[1]) * (decay_ref[...] * LOG2E)
    lead_ref[group] = lead
    lead_t_ref[group] = lead.T
    step_t_ref[group] = step.T


def mix_group(group, heads, tiles, x_ref, xb_ref, y_ref, gram_ref, lead_ref, lead_t_ref, step_t_ref):
    rows = gram_ref.shape[2]
    channels = xb_ref.shape[1]
    base = pl.ds(pl.multiple_of(group * rows, rows), rows)
    for tile in tiles:
        xb_ref[base, pl.ds(tile * 128, 128)] = x_ref[tile, base, :].astype(BF16)
    i = lax.broadcasted_iota(jnp.int32, (rows, rows), 0)
    j = lax.broadcasted_iota(jnp.int32, (rows, rows), 1)
    causal = j <= i
    for head in heads:
        back = HEADS + head
        gap = jnp.where(
            causal,
            lead_t_ref[group, head : head + 1, :] - lead_ref[group, :, head : head + 1],
            lead_t_ref[group, back : back + 1, :] - lead_ref[group, :, back : back + 1],
        )
        weight = jnp.exp2(jnp.minimum(gap, 0.0)) * (
            gram_ref[group, 0] * step_t_ref[group, head : head + 1, :]
            + gram_ref[group, 1] * step_t_ref[group, back : back + 1, :]
        )
        start, offset = window_of(head, channels)
        normed = xb_ref[base, pl.ds(start, WINDOW)]
        mixed = jnp.dot(weight.astype(BF16), normed, preferred_element_type=F32) + normed.astype(F32)
        mask = head_mask(rows, offset)
        for side in range(WINDOW // 128):
            own = slice(side * 128, side * 128 + 128)
            if offset < own.stop and offset + HEAD > own.start:
                place = (start // 128 + side, base, slice(None))
                y_ref[place] = jnp.where(mask[:, own], mixed[:, own], y_ref[place])


def kernel(
    frames, chunks,
    q_hbm, k_hbm, v_hbm, sw_hbm, tw_hbm, gain_ref, bias_ref, decay_ref, o_ref,
    q_ref, k_ref, v_ref, sw_ref, tw_ref, acc_ref, out1_ref, in1_ref, x_ref, xb_ref, y_ref, proj_ref,
    gram_ref, lead_ref, lead_t_ref, step_t_ref, out2_ref,
    q_sem, in_sem, send1, recv1, send2, recv2, own_sem,
):
    video, me = lax.axis_index("video"), lax.axis_index("seq")
    tokens, channels = out1_ref.shape
    per = tokens // frames
    ring = frames // 2
    my_ring, my_side = me // 2, lax.rem(me, 2)
    block = acc_ref.shape[0]
    tiles = channels // 128

    half = ring // 2
    my_parity = lax.rem(my_ring, 2)

    def shift(place):
        return half + jnp.where(lax.rem(place, 2) == 0, place // 2, -((place + 1) // 2))

    def device_at(distance, side):
        return 2 * lax.rem(my_ring + distance, ring) + side

    def peer(n):
        return device_at(shift(n // 2), lax.rem(n, 2))

    def slot_at(distance):
        back = lax.rem(ring - distance, ring)
        place = jnp.where(back >= half, 2 * (back - half), 2 * (half - back) - 1)
        return 2 * place + my_side

    def first_shift(place):
        step = lax.rem(place, half)
        up = lax.rem(step + place // half + my_parity, 2) == 0
        return jnp.where(up, half + step, half - 1 - step)

    def rows_of(index):
        return pl.ds(pl.multiple_of(index * per, per), per)

    def load_queries(place):
        rows = 2 * per
        source = lax.rem(my_ring + first_shift(place), ring)
        return pltpu.make_async_copy(
            q_hbm.at[pl.ds(pl.multiple_of(source * rows, rows), rows)],
            q_ref.at[pl.ds(pl.multiple_of(place * rows, rows), rows)],
            q_sem.at[place],
        )

    def each(low, high, body):
        def step(n, carry):
            body(n)
            return carry

        lax.fori_loop(low, high, step, 0)

    loads = [
        pltpu.make_async_copy(source, target, in_sem.at[n])
        for n, (source, target) in enumerate(
            ((k_hbm, k_ref), (v_hbm, v_ref), (sw_hbm, sw_ref), (tw_hbm, tw_ref))
        )
    ]
    barrier = pltpu.get_barrier_semaphore()

    def greet(k):
        pl.semaphore_signal(
            barrier, inc=1, device_id=(video, lax.rem(me + k, frames)), device_id_type=MESH
        )

    loads[0].start()
    each(half, frames - half, greet)
    each(0, ring, lambda place: load_queries(place).start())
    for load in loads[1:]:
        load.start()
    each(1, half, greet)
    each(frames - half, frames, greet)
    each(0, ring, lambda place: load_queries(place).wait())
    for load in loads[:2]:
        load.wait()

    def first_copy(n):
        distance = first_shift(n // 2)
        there = slot_at(distance)
        return pltpu.make_async_remote_copy(
            src_ref=out1_ref.at[rows_of(n)],
            dst_ref=in1_ref.at[rows_of(there)],
            send_sem=send1.at[n],
            recv_sem=recv1.at[there],
            device_id=(video, device_at(distance, lax.rem(n, 2))),
            device_id_type=MESH,
        )

    def first_arrival(n):
        return pltpu.make_async_remote_copy(
            src_ref=out1_ref.at[rows_of(n)],
            dst_ref=in1_ref.at[rows_of(n)],
            send_sem=send1.at[n],
            recv_sem=recv1.at[n],
            device_id=(video, peer(n)),
            device_id_type=MESH,
        )

    own_slot = frames - 2 + my_side
    own_first = 2 * (half * my_parity + half - 1) + my_side

    def remote(n, action, own=own_slot):
        @pl.when(n != own)
        def _():
            action(n)

    def remote_first(n, action):
        remote(n, action, own_first)

    per_block = block // per

    def first_part(turn):
        row = pl.multiple_of(turn * block, block)
        attend(q_ref, k_ref, v_ref, acc_ref, row)
        out1_ref[pl.ds(row, block), :] = normalize(acc_ref[...], gain_ref[...][None])

        @pl.when(turn == 0)
        def _():
            pl.semaphore_wait(barrier, frames - 1)

        each(turn * per_block, (turn + 1) * per_block, lambda n: remote_first(n, lambda n: first_copy(n).start()))

    each(0, tokens // block, first_part)
    in1_ref[rows_of(own_slot), :] = out1_ref[rows_of(own_first), :]

    groups, rows = gram_ref.shape[0], gram_ref.shape[2]

    def arrive(batch):
        for k in range(rows // per):
            n = batch * (rows // per) + k
            remote(n, lambda n: first_arrival(n).wait_recv())
        arrived = in1_ref[pl.ds(pl.multiple_of(batch * rows, rows), rows), :]
        state = jnp.dot(arrived, sw_ref[...], preferred_element_type=F32).astype(BF16).astype(F32)
        step = lax.dot_general(arrived, tw_ref[...], NT, preferred_element_type=F32).astype(BF16).astype(F32)
        for k in range(rows // per):
            n = batch * (rows // per) + k
            place = pl.ds(peer(n), per, stride=frames)
            here = slice(k * per, k * per + per)
            wide = in1_ref[rows_of(n), :].astype(F32)
            for tile in range(tiles):
                x_ref[tile, place, :] = wide[:, tile * 128 : tile * 128 + 128]
            proj_ref[0, place, :] = state[here, :128]
            proj_ref[1, place, :] = state[here, 128:]
            proj_ref[2, place, :] = jnp.concatenate([step[here]] * (128 // step.shape[1]), axis=1)

    for load in loads[2:]:
        load.wait()
    each(0, groups, arrive)
    each(
        0,
        groups,
        lambda group: prepare_group(
            group, proj_ref, bias_ref, decay_ref, gram_ref, lead_ref, lead_t_ref, step_t_ref
        ),
    )

    def second_copy(c, n):
        lanes = pl.ds(chunks[c][0], chunks[c][1])
        return pltpu.make_async_remote_copy(
            src_ref=out2_ref.at[rows_of(n), lanes],
            dst_ref=o_ref.at[rows_of(me), lanes],
            send_sem=send2.at[c, n],
            recv_sem=recv2.at[c, slot_at(shift(n // 2))],
            device_id=(video, peer(n)),
            device_id_type=MESH,
        )

    def second_arrival(c, n):
        lanes = pl.ds(chunks[c][0], chunks[c][1])
        return pltpu.make_async_remote_copy(
            src_ref=out2_ref.at[rows_of(n), lanes],
            dst_ref=o_ref.at[rows_of(peer(n)), lanes],
            send_sem=send2.at[c, n],
            recv_sem=recv2.at[c, n],
            device_id=(video, peer(n)),
            device_id_type=MESH,
        )

    done, wide_done = 0, 0
    for c, (first, width) in enumerate(chunks):
        until = -(-(first + width) // HEAD)
        wide_until = (window_of(until - 1, channels)[0] + WINDOW) // 128
        heads, wide = range(done, until), range(wide_done, wide_until)
        done, wide_done = until, wide_until
        each(
            0,
            groups,
            lambda group, heads=heads, wide=wide: mix_group(
                group, heads, wide, x_ref, xb_ref, y_ref, gram_ref, lead_ref, lead_t_ref, step_t_ref
            ),
        )

        def give(n, c=c, first=first, width=width):
            for lane in range(first, first + width, 128):
                out2_ref[rows_of(n), pl.ds(lane, 128)] = y_ref[
                    lane // 128, pl.ds(peer(n), per, stride=frames), :
                ].astype(BF16)
            remote(n, lambda n: second_copy(c, n).start())

        each(0, frames, give)

    own = pltpu.make_async_copy(out2_ref.at[rows_of(own_slot)], o_ref.at[rows_of(me)], own_sem)
    own.start()
    each(0, frames, lambda n: remote_first(n, lambda n: first_copy(n).wait_send()))
    for c in range(len(chunks)):

        def finish(n, c=c):
            second_copy(c, n).wait_send()
            second_arrival(c, n).wait_recv()

        each(0, frames, lambda n, finish=finish: remote(n, finish))
    own.wait()


def shards(queries, key_vectors, values_in, norm_gain, state_weight, step_weight, step_bias, decay_rate):
    tokens, channels = queries.shape
    frames = lax.axis_size("seq")
    rows = 4 * frames
    groups = tokens // rows
    block = tokens // 2
    chunks = ((0, 128), (128, 256), (384, 384), (768, 384))
    vmem = pl.BlockSpec(memory_space=pltpu.VMEM)
    hbm = pl.BlockSpec(memory_space=pltpu.HBM)
    return pl.pallas_call(
        functools.partial(kernel, frames, chunks),
        out_shape=pltpu.VMEM((tokens, channels), BF16),
        in_specs=[hbm, hbm, hbm, hbm, hbm, vmem, vmem, vmem],
        out_specs=pl.BlockSpec(memory_space=pltpu.VMEM),
        scratch_shapes=[
            pltpu.VMEM((tokens, channels), BF16),
            pltpu.VMEM((tokens, channels), BF16),
            pltpu.VMEM((tokens, channels), BF16),
            pltpu.VMEM(state_weight.shape, BF16),
            pltpu.VMEM(step_weight.shape[::-1], BF16),
            pltpu.VMEM((block, channels), F32),
            pltpu.VMEM((tokens, channels), BF16),
            pltpu.VMEM((tokens, channels), BF16),
            pltpu.VMEM((channels // 128, tokens, 128), F32),
            pltpu.VMEM((tokens, channels), BF16),
            pltpu.VMEM((channels // 128, tokens, 128), F32),
            pltpu.VMEM((3, tokens, 128), F32),
            pltpu.VMEM((groups, 2, rows, rows), F32),
            pltpu.VMEM((groups, rows, 2 * HEADS), F32),
            pltpu.VMEM((groups, 2 * HEADS, rows), F32),
            pltpu.VMEM((groups, 2 * HEADS, rows), F32),
            pltpu.VMEM((tokens, channels), BF16),
            pltpu.SemaphoreType.DMA((frames // 2,)),
            pltpu.SemaphoreType.DMA((4,)),
            pltpu.SemaphoreType.DMA((frames,)),
            pltpu.SemaphoreType.DMA((frames,)),
            pltpu.SemaphoreType.DMA((len(chunks), frames)),
            pltpu.SemaphoreType.DMA((len(chunks), frames)),
            pltpu.SemaphoreType.DMA,
        ],
        compiler_params=pltpu.CompilerParams(
            collective_id=0, has_side_effects=True, vmem_limit_bytes=56 * 2**20
        ),
    )(
        queries, key_vectors, values_in, state_weight, step_weight.T, norm_gain, step_bias[None], decay_rate[None]
    )


def solution(mesh):
    rows = P(("video", "seq"), None)
    return jax.shard_map(
        shards,
        mesh=mesh,
        in_specs=(rows, rows, rows, P(), P(), P(), P(), P()),
        out_specs=rows,
        check_vma=False,
    )
```

```python
import functools

import jax
import jax.numpy as jnp
from jax import lax
from jax.experimental import pallas as pl
from jax.experimental.pallas import tpu as pltpu
from jax.sharding import PartitionSpec as P

HEADS = 16
HEAD = 72
STATE = 64
EPSILON = 1e-06
LOG2E = 1.4426950408889634
WINDOW = 256
MESH = pl.DeviceIdType.MESH
NT = (((1,), (1,)), ((), ()))
F32 = jnp.float32
BF16 = jnp.bfloat16


def window_of(head, channels):
    start = min(head * HEAD // 128 * 128, channels - WINDOW)
    return start, head * HEAD - start


def head_mask(rows, offset):
    lane = lax.broadcasted_iota(jnp.int32, (rows, WINDOW), 1)
    return (lane >= offset) & (lane < offset + HEAD)


def attend(heads, q_ref, k_ref, v_ref, acc_ref, row):
    rows, channels = acc_ref.shape
    scale = HEAD ** (-0.5) * LOG2E
    for head in heads:
        start, offset = window_of(head, channels)
        lanes = pl.ds(start, WINDOW)
        mask = head_mask(rows, offset)
        query = jnp.where(mask, q_ref[pl.ds(row, rows), lanes], jnp.zeros((), BF16))
        scores = lax.dot_general(query, k_ref[:, lanes], NT, preferred_element_type=F32)
        row_max = jnp.max(scores, axis=1, keepdims=True)
        exponent = jnp.exp2((scores - row_max) * scale)
        total = jnp.sum(exponent, axis=1, keepdims=True)
        probabilities = (exponent * (1.0 / total)).astype(BF16)
        mixed = jnp.dot(probabilities, v_ref[:, lanes], preferred_element_type=F32)
        acc_ref[:, lanes] = jnp.where(mask, mixed, acc_ref[:, lanes])


def normalize(attended, gain):
    widened = attended.astype(BF16).astype(F32)
    mean_square = jnp.mean(widened * widened, axis=1, keepdims=True)
    return (widened * lax.rsqrt(mean_square + EPSILON) * gain).astype(BF16)


def prepare_group(group, proj_ref, bias_ref, decay_ref, gram_ref, lead_ref, lead_t_ref, step_t_ref):
    rows = gram_ref.shape[2]
    frames = rows // 4
    base = pl.ds(group * rows if isinstance(group, int) else pl.multiple_of(group * rows, rows), rows)
    i = lax.broadcasted_iota(jnp.int32, (rows, rows), 0)
    j = lax.broadcasted_iota(jnp.int32, (rows, rows), 1)
    same = (i // frames) == (j // frames)
    causal, anti = same & (j <= i), same & (j >= i)
    for direction, mask in ((0, causal), (1, anti)):
        state = proj_ref[direction, base, :].astype(BF16)
        gram = lax.dot_general(state[:, STATE:], state[:, :STATE], NT, preferred_element_type=F32)
        gram_ref[group, direction] = jnp.where(mask, gram * STATE ** (-0.5), 0.0)
    step = proj_ref[2, base, : 2 * HEADS] + bias_ref[...]
    step = jnp.maximum(step, 0.0) + jnp.log1p(jnp.exp(-jnp.abs(step)))
    high = step.astype(BF16)
    low = (step - high.astype(F32)).astype(BF16)
    sums = []
    for mask in (causal, anti):
        ones = jnp.where(mask, 1.0, 0.0).astype(BF16)
        sums.append(
            jnp.dot(ones, high, preferred_element_type=F32) + jnp.dot(ones, low, preferred_element_type=F32)
        )
    column = lax.broadcasted_iota(jnp.int32, step.shape, 1)
    lead = jnp.where(column < HEADS, sums[0], sums[1]) * (decay_ref[...] * LOG2E)
    lead_ref[group] = lead
    lead_t_ref[group] = lead.T
    step_t_ref[group] = step.T


def mix_group(group, heads, tiles, x_ref, xb_ref, y_ref, gram_ref, lead_ref, lead_t_ref, step_t_ref):
    rows = gram_ref.shape[2]
    channels = xb_ref.shape[1]
    base = pl.ds(group * rows if isinstance(group, int) else pl.multiple_of(group * rows, rows), rows)
    for tile in tiles:
        xb_ref[base, pl.ds(tile * 128, 128)] = x_ref[tile, base, :].astype(BF16)
    i = lax.broadcasted_iota(jnp.int32, (rows, rows), 0)
    j = lax.broadcasted_iota(jnp.int32, (rows, rows), 1)
    causal = j <= i
    for head in heads:
        back = HEADS + head
        gap = jnp.where(
            causal,
            lead_t_ref[group, head : head + 1, :] - lead_ref[group, :, head : head + 1],
            lead_t_ref[group, back : back + 1, :] - lead_ref[group, :, back : back + 1],
        )
        weight = jnp.exp2(jnp.minimum(gap, 0.0)) * (
            gram_ref[group, 0] * step_t_ref[group, head : head + 1, :]
            + gram_ref[group, 1] * step_t_ref[group, back : back + 1, :]
        )
        start, offset = window_of(head, channels)
        normed = xb_ref[base, pl.ds(start, WINDOW)]
        mixed = jnp.dot(weight.astype(BF16), normed, preferred_element_type=F32) + normed.astype(F32)
        mask = head_mask(rows, offset)
        for side in range(WINDOW // 128):
            own = slice(side * 128, side * 128 + 128)
            if offset < own.stop and offset + HEAD > own.start:
                place = (start // 128 + side, base, slice(None))
                y_ref[place] = jnp.where(mask[:, own], mixed[:, own], y_ref[place])


def kernel(
    frames, firsts, chunks,
    q_hbm, k_hbm, v_hbm, sw_hbm, tw_hbm, gain_ref, bias_ref, decay_ref, o_ref,
    q_ref, k_ref, v_ref, sw_ref, tw_ref, acc_ref, out1_ref, in1_ref, x_ref, xb_ref, y_ref, proj_ref,
    gram_ref, lead_ref, lead_t_ref, step_t_ref, out2_ref,
    q_sem, in_sem, send1, recv1, send2, recv2, own_sem,
):
    video, me = lax.axis_index("video"), lax.axis_index("seq")
    tokens, channels = out1_ref.shape
    per = tokens // frames
    ring = frames // 2
    my_ring, my_side = me // 2, lax.rem(me, 2)
    block = acc_ref.shape[0]
    tiles = channels // 128

    half = ring // 2

    def shift(place):
        return half + jnp.where(lax.rem(place, 2) == 0, place // 2, -((place + 1) // 2))

    def device_at(distance, side):
        return 2 * lax.rem(my_ring + distance, ring) + side

    def peer(n):
        return device_at(shift(n // 2), lax.rem(n, 2))

    def slot_at(distance):
        back = lax.rem(ring - distance, ring)
        place = jnp.where(back >= half, 2 * (back - half), 2 * (half - back) - 1)
        return 2 * place + my_side

    def first_target(n):
        distance = shift(lax.rem(n, ring))
        place = lax.rem(my_ring + distance, ring)
        return distance, 2 * place + lax.rem(place + n // ring, 2)

    def rows_of(index):
        return pl.ds(pl.multiple_of(index * per, per), per)

    def load_queries(n):
        return pltpu.make_async_copy(
            q_hbm.at[rows_of(first_target(n)[1])], q_ref.at[rows_of(n)], q_sem.at[n]
        )

    def each(low, high, body):
        def step(n, carry):
            body(n)
            return carry

        lax.fori_loop(low, high, step, 0)

    loads = [
        pltpu.make_async_copy(source, target, in_sem.at[n])
        for n, (source, target) in enumerate(
            ((k_hbm, k_ref), (v_hbm, v_ref), (sw_hbm, sw_ref), (tw_hbm, tw_ref))
        )
    ]
    barrier = pltpu.get_barrier_semaphore()

    def greet(k):
        pl.semaphore_signal(
            barrier, inc=1, device_id=(video, lax.rem(me + k, frames)), device_id_type=MESH
        )

    loads[0].start()
    each(half, frames - half, greet)
    each(0, ring, lambda n: load_queries(n).start())
    loads[1].start()
    each(ring, frames, lambda n: load_queries(n).start())
    for load in loads[2:]:
        load.start()
    each(1, half, greet)
    each(frames - half, frames, greet)
    for load in loads[:2]:
        load.wait()

    def first_copy(c, n):
        distance, target = first_target(n)
        there = slot_at(distance)
        lanes = pl.ds(firsts[c][0], firsts[c][1])
        return pltpu.make_async_remote_copy(
            src_ref=out1_ref.at[rows_of(n), lanes],
            dst_ref=in1_ref.at[rows_of(there), lanes],
            send_sem=send1.at[c, n],
            recv_sem=recv1.at[c, there],
            device_id=(video, target),
            device_id_type=MESH,
        )

    def first_arrival(c, n):
        lanes = pl.ds(firsts[c][0], firsts[c][1])
        return pltpu.make_async_remote_copy(
            src_ref=out1_ref.at[rows_of(n), lanes],
            dst_ref=in1_ref.at[rows_of(n), lanes],
            send_sem=send1.at[c, n],
            recv_sem=recv1.at[c, n],
            device_id=(video, peer(n)),
            device_id_type=MESH,
        )

    own_slot = frames - 2 + my_side
    own_first = lax.rem(my_ring + my_side, 2) * ring + ring - 1

    def remote(n, action, own=own_slot):
        @pl.when(n != own)
        def _():
            action(n)

    def remote_first(n, action):
        remote(n, action, own_first)

    per_block = block // per

    def first_part(turn):
        row = pl.multiple_of(turn * block, block)
        each(turn * ring, (turn + 1) * ring, lambda n: load_queries(n).wait())
        done = 0
        for c, (first, width) in enumerate(firsts):
            until = -(-(first + width) // HEAD)
            attend(range(done, until), q_ref, k_ref, v_ref, acc_ref, row)
            done = until
            lanes = pl.ds(first, width)
            out1_ref[pl.ds(row, block), lanes] = acc_ref[:, lanes].astype(BF16)
            if c == 0:

                @pl.when(turn == 0)
                def _():
                    pl.semaphore_wait(barrier, frames - 1)

            def send(n, c=c):
                remote_first(n, lambda n: first_copy(c, n).start())

            each(turn * per_block, (turn + 1) * per_block, send)

    each(0, tokens // block, first_part)
    in1_ref[rows_of(own_slot), :] = out1_ref[rows_of(own_first), :]

    groups, rows = gram_ref.shape[0], gram_ref.shape[2]

    def arrive(batch):
        for k in range(rows // per):
            n = batch * (rows // per) + k
            for c in range(len(firsts)):
                remote(n, lambda n, c=c: first_arrival(c, n).wait_recv())
        arrived = normalize(in1_ref[pl.ds(pl.multiple_of(batch * rows, rows), rows), :], gain_ref[...][None])
        state = jnp.dot(arrived, sw_ref[...], preferred_element_type=F32).astype(BF16).astype(F32)
        step = lax.dot_general(arrived, tw_ref[...], NT, preferred_element_type=F32).astype(BF16).astype(F32)
        for k in range(rows // per):
            n = batch * (rows // per) + k
            place = pl.ds(peer(n), per, stride=frames)
            here = slice(k * per, k * per + per)
            wide = arrived[here].astype(F32)
            for tile in range(tiles):
                x_ref[tile, place, :] = wide[:, tile * 128 : tile * 128 + 128]
            proj_ref[0, place, :] = state[here, :128]
            proj_ref[1, place, :] = state[here, 128:]
            proj_ref[2, place, :] = jnp.concatenate([step[here]] * (128 // step.shape[1]), axis=1)

    for load in loads[2:]:
        load.wait()
    each(0, groups, arrive)
    for group in range(groups):
        prepare_group(group, proj_ref, bias_ref, decay_ref, gram_ref, lead_ref, lead_t_ref, step_t_ref)

    def second_copy(c, n):
        lanes = pl.ds(chunks[c][0], chunks[c][1])
        return pltpu.make_async_remote_copy(
            src_ref=out2_ref.at[rows_of(n), lanes],
            dst_ref=o_ref.at[rows_of(me), lanes],
            send_sem=send2.at[c, n],
            recv_sem=recv2.at[c, slot_at(shift(n // 2))],
            device_id=(video, peer(n)),
            device_id_type=MESH,
        )

    def second_arrival(c, n):
        lanes = pl.ds(chunks[c][0], chunks[c][1])
        return pltpu.make_async_remote_copy(
            src_ref=out2_ref.at[rows_of(n), lanes],
            dst_ref=o_ref.at[rows_of(peer(n)), lanes],
            send_sem=send2.at[c, n],
            recv_sem=recv2.at[c, n],
            device_id=(video, peer(n)),
            device_id_type=MESH,
        )

    done, wide_done = 0, 0
    for c, (first, width) in enumerate(chunks):
        until = -(-(first + width) // HEAD)
        wide_until = (window_of(until - 1, channels)[0] + WINDOW) // 128
        heads, wide = range(done, until), range(wide_done, wide_until)
        done, wide_done = until, wide_until

        def mix(group, heads=heads, wide=wide):
            mix_group(
                group, heads, wide, x_ref, xb_ref, y_ref, gram_ref, lead_ref, lead_t_ref, step_t_ref
            )

        if c == 0:
            for group in range(groups):
                mix(group)
        else:
            each(0, groups, mix)

        def give(n, c=c, first=first, width=width):
            for lane in range(first, first + width, 128):
                out2_ref[rows_of(n), pl.ds(lane, 128)] = y_ref[
                    lane // 128, pl.ds(peer(n), per, stride=frames), :
                ].astype(BF16)
            remote(n, lambda n: second_copy(c, n).start())

        each(0, frames, give)

    own = pltpu.make_async_copy(out2_ref.at[rows_of(own_slot)], o_ref.at[rows_of(me)], own_sem)
    own.start()
    for c in range(len(firsts)):
        each(0, frames, lambda n, c=c: remote_first(n, lambda n: first_copy(c, n).wait_send()))
    for c in range(len(chunks)):

        def finish(n, c=c):
            second_copy(c, n).wait_send()
            second_arrival(c, n).wait_recv()

        each(0, frames, lambda n, finish=finish: remote(n, finish))
    own.wait()


def shards(queries, key_vectors, values_in, norm_gain, state_weight, step_weight, step_bias, decay_rate):
    tokens, channels = queries.shape
    frames = lax.axis_size("seq")
    rows = 4 * frames
    groups = tokens // rows
    block = tokens // 2
    firsts = ((0, 640), (640, 512))
    chunks = ((0, 128), (128, 256), (384, 384), (768, 384))
    vmem = pl.BlockSpec(memory_space=pltpu.VMEM)
    hbm = pl.BlockSpec(memory_space=pltpu.HBM)
    return pl.pallas_call(
        functools.partial(kernel, frames, firsts, chunks),
        out_shape=pltpu.VMEM((tokens, channels), BF16),
        in_specs=[hbm, hbm, hbm, hbm, hbm, vmem, vmem, vmem],
        out_specs=pl.BlockSpec(memory_space=pltpu.VMEM),
        scratch_shapes=[
            pltpu.VMEM((tokens, channels), BF16),
            pltpu.VMEM((tokens, channels), BF16),
            pltpu.VMEM((tokens, channels), BF16),
            pltpu.VMEM(state_weight.shape, BF16),
            pltpu.VMEM(step_weight.shape[::-1], BF16),
            pltpu.VMEM((block, channels), F32),
            pltpu.VMEM((tokens, channels), BF16),
            pltpu.VMEM((tokens, channels), BF16),
            pltpu.VMEM((channels // 128, tokens, 128), F32),
            pltpu.VMEM((tokens, channels), BF16),
            pltpu.VMEM((channels // 128, tokens, 128), F32),
            pltpu.VMEM((3, tokens, 128), F32),
            pltpu.VMEM((groups, 2, rows, rows), F32),
            pltpu.VMEM((groups, rows, 2 * HEADS), F32),
            pltpu.VMEM((groups, 2 * HEADS, rows), F32),
            pltpu.VMEM((groups, 2 * HEADS, rows), F32),
            pltpu.VMEM((tokens, channels), BF16),
            pltpu.SemaphoreType.DMA((frames,)),
            pltpu.SemaphoreType.DMA((4,)),
            pltpu.SemaphoreType.DMA((len(firsts), frames)),
            pltpu.SemaphoreType.DMA((len(firsts), frames)),
            pltpu.SemaphoreType.DMA((len(chunks), frames)),
            pltpu.SemaphoreType.DMA((len(chunks), frames)),
            pltpu.SemaphoreType.DMA,
        ],
        compiler_params=pltpu.CompilerParams(
            collective_id=0, has_side_effects=True, vmem_limit_bytes=56 * 2**20
        ),
    )(
        queries, key_vectors, values_in, state_weight, step_weight.T, norm_gain, step_bias[None], decay_rate[None]
    )


def solution(mesh):
    rows = P(("video", "seq"), None)
    return jax.shard_map(
        shards,
        mesh=mesh,
        in_specs=(rows, rows, rows, P(), P(), P(), P(), P()),
        out_specs=rows,
        check_vma=False,
    )
```
